32 devices in a mesh: blk: 8 (over z, y), uly: 4 (over x, core).
Axes of the slice: x: 2, y: 2, z: 4, core: 2. Of those that a mesh axis runs over, the one named last changes fastest.
Arguments:
- queries: bfloat16 [1536, 2560], P(('blk', 'uly')), may hold values from -30 to 30
- keys: bfloat16 [1536, 2560], P(('blk', 'uly')), may hold values from -4 to 4
- values: bfloat16 [1536, 2560], P(('blk', 'uly')), may hold values from -6 to 6
Outputs:
- attended: bfloat16 [1536, 2560], P(('blk', 'uly'))
The draws below stay inside these ranges and needn't reach their ends.
All inputs are finite; a program needn't handle non-finite values.
Results may differ from the reference program's by a relative error of at most 0.0049.
Values may be sent and summed in bfloat16 or wider, within the bound.
A program may use at most 192 MiB of HBM per device.

```python
import jax
import jax.numpy as jnp
from jax import lax

HEADS = 20
HEAD_DIM = 128
TOKENS = 1536


def draw_queries(key, part):
    key = jax.random.fold_in(key, 11)
    base = 2.5 * jnp.clip(jax.random.normal(key, (TOKENS, HEADS * HEAD_DIM), jnp.float32), -6.0, 6.0)
    return base.astype(jnp.bfloat16)


def draw_keys(key, part):
    key = jax.random.fold_in(key, 23)
    base = jnp.clip(jax.random.normal(key, (TOKENS, HEADS * HEAD_DIM), jnp.float32), -4.0, 4.0)
    return base.astype(jnp.bfloat16)


def shard_levels(key, shape, shards, smallest, largest):
    gain = 1.0
    for position, parts in shards:
        draws = jax.random.uniform(jax.random.fold_in(jax.random.fold_in(key, 6), position), (parts,), jnp.float32, smallest / len(shards), largest / len(shards))
        gain = gain * jnp.repeat(jnp.exp(draws), shape[position] // parts).reshape((-1,) + (1,) * (len(shape) - 1 - position))
    return gain


def noise(own_key, dims, width, reach, shards=(), kind=jnp.bfloat16):
    drawn = width * jax.random.normal(own_key, dims, jnp.float32)
    if shards:
        drawn = drawn * shard_levels(own_key, dims, shards, -0.22, 0.18)
    return jnp.clip(drawn, -reach, reach).astype(kind)


def setup_inputs(seed: int = 0) -> dict:
    streams_of = jax.random.split(jax.random.key(seed), 4)
    queries = draw_queries(jax.random.fold_in(streams_of[3], 71), 0)
    keys = draw_keys(jax.random.fold_in(streams_of[3], 71), 0)
    values = noise(streams_of[2], (TOKENS, HEADS * HEAD_DIM), 1.0, 6.0, ((0, 32),))
    return {"queries": queries, "keys": keys, "values": values}


def one_head(operands):
    query, key, value = operands
    scores = jnp.dot(query, key.T, preferred_element_type=jnp.float32) * (1.0 / jnp.sqrt(jnp.float32(query.shape[1])))
    probs = jnp.exp(scores - lax.optimization_barrier(jnp.max(scores, axis=1, keepdims=True)))
    total = lax.optimization_barrier(jnp.sum(probs, axis=1, keepdims=True))
    weights = probs.astype(jnp.bfloat16)
    summed = jnp.dot(weights, value, preferred_element_type=jnp.float32)
    return (summed / total).astype(jnp.bfloat16)

def reference(queries, keys, values):

    def split_heads(array):
        return jnp.transpose(array.reshape(TOKENS, HEADS, HEAD_DIM), (1, 0, 2))
    stacked = lax.map(one_head, (split_heads(queries), split_heads(keys), split_heads(values)))
    return jnp.transpose(stacked, (1, 0, 2)).reshape(TOKENS, HEADS * HEAD_DIM)
```

```python
import functools

import jax
import jax.numpy as jnp
from jax import lax
from jax.experimental import pallas as pl
from jax.experimental.pallas import tpu as pltpu
from jax.sharding import PartitionSpec as P

HEAD_DIM = 128
GROUPS = 4
MESH = pl.DeviceIdType.MESH
LOG2E = 1.4426950408889634


def attend_kernel(q_in, k_in, v_in, out, q_buf, kv, acc, tot, top, o_buf, z_send, q_recv, z_recv,
                  x_send, x_recv, y_send, y_recv, s_send, s_recv, d_send, dk_recv, dv_recv,
                  own_sem, o_send, o_recv):
    rows, features = q_in.shape
    cols = features // GROUPS
    heads = cols // HEAD_DIM
    b, u = lax.axis_index("blk"), lax.axis_index("uly")
    z, y = b // 2, b % 2
    x, c = u // 2, u % 2

    def plane(j):
        return lax.rem(z + j + GROUPS, GROUPS)

    def column(index):
        return pl.ds(pl.multiple_of(index * cols, HEAD_DIM), cols)

    x_peer = (b, 2 * (1 - x) + c)
    y_peer = (2 * z + 1 - y, u)
    sibling = (b, 2 * x + 1 - c)

    def z_peer(j):
        return (2 * plane(j) + y, u)

    barrier = pltpu.get_barrier_semaphore()
    peers = [z_peer(1), z_peer(2), z_peer(3), x_peer, y_peer, sibling]
    for peer in peers:
        pl.semaphore_signal(barrier, inc=1, device_id=peer, device_id_type=MESH)
    pl.semaphore_wait(barrier, len(peers))

    sends = []

    def send(src, dst, send_sem, recv_sem, peer):
        copy = pltpu.make_async_remote_copy(
            src_ref=src, dst_ref=dst, send_sem=send_sem, recv_sem=recv_sem,
            device_id=peer, device_id_type=MESH)
        copy.start()
        sends.append(copy)

    def landed(ref, sem):
        pltpu.make_async_copy(ref, ref, sem).wait()

    def slot(s):
        return pl.ds(s * rows, rows)

    for j in range(1, GROUPS):
        to = column(plane(j))
        send(q_in.at[:, to], q_buf.at[slot(j)], z_send.at[3 * j], q_recv.at[j], z_peer(j))
        send(k_in.at[:, to], kv.at[j, 0, slot(0)], z_send.at[3 * j + 1], z_recv.at[j], z_peer(j))
        send(v_in.at[:, to], kv.at[j, 1, slot(0)], z_send.at[3 * j + 2], z_recv.at[j], z_peer(j))
    mine = column(z)
    own = [
        pltpu.make_async_copy(q_in.at[:, mine], q_buf.at[slot(0)], own_sem.at[0]),
        pltpu.make_async_copy(k_in.at[:, mine], kv.at[0, 0, slot(0)], own_sem.at[1]),
        pltpu.make_async_copy(v_in.at[:, mine], kv.at[0, 1, slot(0)], own_sem.at[2]),
    ]
    for copy in own:
        copy.start()

    def stage1(j):
        if j == 0:
            for copy in own:
                copy.wait()
        else:
            landed(kv.at[j, :, slot(0)], z_recv.at[j])
        block = kv.at[j, :, slot(0)]
        send(block, kv.at[j, :, slot(1)], x_send.at[j], x_recv.at[j], x_peer)
        send(block, kv.at[j, :, slot(2)], y_send.at[j], y_recv.at[j], y_peer)
        send(block, kv.at[j, :, slot(4)], s_send.at[4 * j], s_recv.at[j], sibling)

    def stage2(j):
        landed(kv.at[j, :, slot(1)], x_recv.at[j])
        send(kv.at[j, 0, slot(1)], kv.at[j, 0, slot(3)], d_send.at[2 * j], dk_recv.at[j], y_peer)
        send(kv.at[j, :, slot(1)], kv.at[j, :, slot(5)], s_send.at[4 * j + 1], s_recv.at[j], sibling)
        landed(kv.at[j, :, slot(2)], y_recv.at[j])
        send(kv.at[j, 1, slot(2)], kv.at[j, 1, slot(3)], d_send.at[2 * j + 1], dv_recv.at[j], x_peer)
        send(kv.at[j, :, slot(2)], kv.at[j, :, slot(6)], s_send.at[4 * j + 2], s_recv.at[j], sibling)

    def stage3(j):
        landed(kv.at[j, 0, slot(3)], dk_recv.at[j])
        landed(kv.at[j, 1, slot(3)], dv_recv.at[j])
        send(kv.at[j, :, slot(3)], kv.at[j, :, slot(7)], s_send.at[4 * j + 3], s_recv.at[j], sibling)

    def fold(j):
        if j == 0:
            for i in range(1, GROUPS):
                landed(q_buf.at[slot(i)], q_recv.at[i])
        landed(kv.at[j, :, pl.ds(4 * rows, 4 * rows)], s_recv.at[j])
        for h in range(heads):
            lanes = slice(h * HEAD_DIM, (h + 1) * HEAD_DIM)
            scores = lax.dot_general(
                q_buf[:, lanes], kv[j, 0, :, lanes], (((1,), (1,)), ((), ())),
                preferred_element_type=jnp.float32) * (LOG2E * HEAD_DIM ** -0.5)
            peak = jnp.max(scores, axis=1, keepdims=True)
            if j > 0:
                before = top[:, h:h + 1]
                peak = jnp.maximum(before, peak)
                shrink = jnp.exp2(before - peak)
            probs = jnp.exp2(scores - peak)
            part = jnp.sum(probs, axis=1, keepdims=True)
            added = jnp.dot(probs.astype(jnp.bfloat16), kv[j, 1, :, lanes],
                            preferred_element_type=jnp.float32)
            if j > 0:
                part = part + shrink * tot[:, h:h + 1]
                added = added + shrink * acc[:, lanes]
            if j < GROUPS - 1:
                top[:, h:h + 1] = peak
                tot[:, h:h + 1] = part
                acc[:, lanes] = added
            else:
                o_buf[:, lanes] = (added / part).astype(jnp.bfloat16)

    stage1(0)
    stage2(0)
    stage1(1)
    stage3(0)
    stage2(1)
    fold(0)
    stage1(2)
    stage3(1)
    stage2(2)
    fold(1)
    stage1(3)
    stage3(2)
    stage2(3)
    fold(2)
    stage3(3)
    fold(3)

    for j in range(1, GROUPS):
        send(o_buf.at[slot(j)], out.at[:, mine], o_send.at[j], o_recv.at[j], z_peer(-j))
    keep = pltpu.make_async_copy(o_buf.at[slot(0)], out.at[:, mine], own_sem.at[0])
    keep.start()
    keep.wait()
    for j in range(1, GROUPS):
        landed(out.at[:, column(plane(j))], o_recv.at[j])
    for copy in sends:
        copy.wait_send()


def attend(queries, keys, values):
    rows, features = queries.shape
    cols = features // GROUPS
    heads = cols // HEAD_DIM
    queries_here = GROUPS * rows
    dma = pltpu.SemaphoreType.DMA
    flops = 4 * queries_here * cols * 32 * rows
    return pl.pallas_call(
        attend_kernel,
        out_shape=jax.ShapeDtypeStruct((rows, features), jnp.bfloat16),
        in_specs=[pl.BlockSpec(memory_space=pl.ANY)] * 3,
        out_specs=pl.BlockSpec(memory_space=pl.ANY),
        scratch_shapes=[
            pltpu.VMEM((queries_here, cols), jnp.bfloat16),
            pltpu.VMEM((GROUPS, 2, 8 * rows, cols), jnp.bfloat16),
            pltpu.VMEM((queries_here, cols), jnp.float32),
            pltpu.VMEM((queries_here, HEAD_DIM), jnp.float32),
            pltpu.VMEM((queries_here, HEAD_DIM), jnp.float32),
            pltpu.VMEM((queries_here, cols), jnp.bfloat16),
            dma((12,)), dma((4,)), dma((4,)),
            dma((4,)), dma((4,)), dma((4,)), dma((4,)),
            dma((16,)), dma((4,)), dma((8,)), dma((4,)), dma((4,)),
            dma((3,)), dma((4,)), dma((4,)),
        ],
        compiler_params=pltpu.CompilerParams(
            collective_id=0, has_side_effects=True, vmem_limit_bytes=40 * 2**20),
        cost_estimate=pl.CostEstimate(flops=flops, bytes_accessed=8 * rows * features, transcendentals=0),
    )(queries, keys, values)


def attend_any(queries, keys, values):
    def to_heads(array):
        return lax.all_to_all(array, "uly", split_axis=1, concat_axis=0, tiled=True)

    heads_q, heads_k, heads_v = to_heads(queries), to_heads(keys), to_heads(values)
    all_k = lax.all_gather(heads_k, "blk", axis=0, tiled=True)
    all_v = lax.all_gather(heads_v, "blk", axis=0, tiled=True)

    def split(array):
        return array.reshape(array.shape[0], -1, HEAD_DIM)

    scores = jnp.einsum("qhd,khd->qhk", split(heads_q), split(all_k),
                        preferred_element_type=jnp.float32) * HEAD_DIM ** (-0.5)
    probs = jnp.exp(scores - jnp.max(scores, axis=2, keepdims=True))
    total = jnp.sum(probs, axis=2)
    summed = jnp.einsum("qhk,khd->qhd", probs.astype(jnp.bfloat16), split(all_v),
                        preferred_element_type=jnp.float32)
    result = (summed / total[:, :, None]).reshape(heads_q.shape).astype(jnp.bfloat16)
    return lax.all_to_all(result, "uly", split_axis=0, concat_axis=1, tiled=True)


def solution(mesh):
    spec = P(("blk", "uly"), None)
    small = mesh.shape["blk"] == 2 * GROUPS and mesh.shape["uly"] == 4
    return jax.shard_map(
        attend if small else attend_any,
        mesh=mesh,
        in_specs=(spec, spec, spec),
        out_specs=spec,
        check_vma=False,
    )
```

```python
import functools

import jax
import jax.numpy as jnp
from jax import lax
from jax.experimental import pallas as pl
from jax.experimental.pallas import tpu as pltpu
from jax.sharding import PartitionSpec as P

HEAD_DIM = 128
GROUPS = 4
MESH = pl.DeviceIdType.MESH
LOG2E = 1.4426950408889634


def attend_kernel(q_in, k_in, v_in, out, q_buf, kv, o_buf, own_sem, z_send, z_recv, q_recv,
                  x_send, x_recv, y_send, y_recv, s_send, s_recv, d_send, dk_recv, dv_recv,
                  o_send, o_recv):
    rows, features = q_in.shape
    cols = features // GROUPS
    heads = cols // HEAD_DIM
    part = GROUPS * rows
    b, u = lax.axis_index("blk"), lax.axis_index("uly")
    z, y = b // 2, b % 2
    x, c = u // 2, u % 2

    def plane(j):
        return lax.rem(z + j + GROUPS, GROUPS)

    def lanes(h):
        return pl.ds(h * HEAD_DIM, HEAD_DIM)

    def column(index, h):
        return pl.ds(pl.multiple_of(index * cols + h * HEAD_DIM, HEAD_DIM), HEAD_DIM)

    def piece(j):
        return pl.ds(j * rows, rows)

    def slot(s):
        return pl.ds(s * part, part)

    x_peer = (b, 2 * (1 - x) + c)
    y_peer = (2 * z + 1 - y, u)
    sibling = (b, 2 * x + 1 - c)

    def z_peer(j):
        return (2 * plane(j) + y, u)

    sends = []

    def send(src, dst, send_sem, recv_sem, peer):
        copy = pltpu.make_async_remote_copy(
            src_ref=src, dst_ref=dst, send_sem=send_sem, recv_sem=recv_sem,
            device_id=peer, device_id_type=MESH)
        copy.start()
        sends.append(copy)

    def landed(ref, sem):
        pltpu.make_async_copy(ref, ref, sem).wait()

    own = []
    for h in range(heads):
        own.append([
            pltpu.make_async_copy(k_in.at[:, column(z, h)], kv.at[0, piece(0), lanes(h)], own_sem.at[3 * h]),
            pltpu.make_async_copy(v_in.at[:, column(z, h)], kv.at[1, piece(0), lanes(h)], own_sem.at[3 * h + 1]),
            pltpu.make_async_copy(q_in.at[:, column(z, h)], q_buf.at[piece(0), lanes(h)], own_sem.at[3 * h + 2]),
        ])
        for copy in own[h]:
            copy.start()

    barrier = pltpu.get_barrier_semaphore()
    peers = [z_peer(1), z_peer(2), z_peer(3), x_peer, y_peer, sibling]
    for peer in peers:
        pl.semaphore_signal(barrier, inc=1, device_id=peer, device_id_type=MESH)
    pl.semaphore_wait(barrier, len(peers))

    for h in range(heads):
        for j in range(1, GROUPS):
            away, base = column(plane(j), h), 9 * h + 3 * (j - 1)
            send(k_in.at[:, away], kv.at[0, piece(j), lanes(h)], z_send.at[base], z_recv.at[h], z_peer(j))
            send(v_in.at[:, away], kv.at[1, piece(j), lanes(h)], z_send.at[base + 1], z_recv.at[h], z_peer(j))
            send(q_in.at[:, away], q_buf.at[piece(j), lanes(h)], z_send.at[base + 2], q_recv.at[h], z_peer(j))

    def stage1(h):
        for copy in own[h]:
            copy.wait()
        landed(kv.at[:, pl.ds(rows, part - rows), lanes(h)], z_recv.at[h])
        block = kv.at[:, slot(0), lanes(h)]
        send(block, kv.at[:, slot(1), lanes(h)], x_send.at[h], x_recv.at[h], x_peer)
        send(block, kv.at[:, slot(2), lanes(h)], y_send.at[h], y_recv.at[h], y_peer)
        send(block, kv.at[:, slot(4), lanes(h)], s_send.at[4 * h], s_recv.at[h], sibling)

    def stage2(h):
        landed(kv.at[:, slot(1), lanes(h)], x_recv.at[h])
        send(kv.at[0, slot(1), lanes(h)], kv.at[0, slot(3), lanes(h)], d_send.at[2 * h], dk_recv.at[h], y_peer)
        send(kv.at[:, slot(1), lanes(h)], kv.at[:, slot(5), lanes(h)], s_send.at[4 * h + 1], s_recv.at[h], sibling)
        landed(kv.at[:, slot(2), lanes(h)], y_recv.at[h])
        send(kv.at[1, slot(2), lanes(h)], kv.at[1, slot(3), lanes(h)], d_send.at[2 * h + 1], dv_recv.at[h], x_peer)
        send(kv.at[:, slot(2), lanes(h)], kv.at[:, slot(6), lanes(h)], s_send.at[4 * h + 2], s_recv.at[h], sibling)

    def stage3(h):
        landed(kv.at[0, slot(3), lanes(h)], dk_recv.at[h])
        landed(kv.at[1, slot(3), lanes(h)], dv_recv.at[h])
        send(kv.at[:, slot(3), lanes(h)], kv.at[:, slot(7), lanes(h)], s_send.at[4 * h + 3], s_recv.at[h], sibling)

    def fold(h):
        landed(q_buf.at[pl.ds(rows, part - rows), lanes(h)], q_recv.at[h])
        landed(kv.at[:, pl.ds(4 * part, 4 * part), lanes(h)], s_recv.at[h])
        scores = lax.dot_general(
            q_buf[:, lanes(h)], kv[0, :, lanes(h)], (((1,), (1,)), ((), ())),
            preferred_element_type=jnp.float32)
        peak = jnp.max(scores, axis=1, keepdims=True)
        probs = jnp.exp2((scores - peak) * (LOG2E * HEAD_DIM ** -0.5))
        total = jnp.sum(probs, axis=1, keepdims=True)
        summed = jnp.dot(probs.astype(jnp.bfloat16), kv[1, :, lanes(h)],
                         preferred_element_type=jnp.float32)
        o_buf[:, lanes(h)] = (summed / total).astype(jnp.bfloat16)
        for j in range(1, GROUPS):
            send(o_buf.at[piece(j), lanes(h)], out.at[:, column(z, h)],
                 o_send.at[3 * h + j - 1], o_recv.at[j - 1], z_peer(-j))
        keep = pltpu.make_async_copy(o_buf.at[piece(0), lanes(h)], out.at[:, column(z, h)], own_sem.at[3 * h])
        keep.start()
        own[h] = [keep]

    for step in range(heads + 3):
        if step < heads:
            stage1(step)
        if 0 <= step - 1 < heads:
            stage2(step - 1)
        if 0 <= step - 2 < heads:
            stage3(step - 2)
        if 0 <= step - 3 < heads:
            fold(step - 3)

    for h in range(heads):
        for copy in own[h]:
            copy.wait()
    for j in range(1, GROUPS):
        block = pl.ds(pl.multiple_of(plane(j) * cols, HEAD_DIM), cols)
        landed(out.at[:, block], o_recv.at[j - 1])
    for copy in sends:
        copy.wait_send()


def attend(queries, keys, values):
    rows, features = queries.shape
    cols = features // GROUPS
    heads = cols // HEAD_DIM
    part = GROUPS * rows
    dma = pltpu.SemaphoreType.DMA
    flops = 4 * part * cols * 8 * part
    return pl.pallas_call(
        attend_kernel,
        out_shape=jax.ShapeDtypeStruct((rows, features), jnp.bfloat16),
        in_specs=[pl.BlockSpec(memory_space=pl.ANY)] * 3,
        out_specs=pl.BlockSpec(memory_space=pl.ANY),
        scratch_shapes=[
            pltpu.VMEM((part, cols), jnp.bfloat16),
            pltpu.VMEM((2, 8 * part, cols), jnp.bfloat16),
            pltpu.VMEM((part, cols), jnp.bfloat16),
            dma((3 * heads,)), dma((9 * heads,)), dma((heads,)), dma((heads,)),
            dma((heads,)), dma((heads,)), dma((heads,)), dma((heads,)),
            dma((4 * heads,)), dma((heads,)), dma((2 * heads,)), dma((heads,)), dma((heads,)),
            dma((3 * heads,)), dma((3,)),
        ],
        compiler_params=pltpu.CompilerParams(
            collective_id=0, has_side_effects=True, vmem_limit_bytes=60 * 2**20),
        cost_estimate=pl.CostEstimate(flops=flops, bytes_accessed=8 * rows * features, transcendentals=0),
    )(queries, keys, values)


def attend_any(queries, keys, values):
    def to_heads(array):
        return lax.all_to_all(array, "uly", split_axis=1, concat_axis=0, tiled=True)

    heads_q, heads_k, heads_v = to_heads(queries), to_heads(keys), to_heads(values)
    all_k = lax.all_gather(heads_k, "blk", axis=0, tiled=True)
    all_v = lax.all_gather(heads_v, "blk", axis=0, tiled=True)

    def split(array):
        return array.reshape(array.shape[0], -1, HEAD_DIM)

    scores = jnp.einsum("qhd,khd->qhk", split(heads_q), split(all_k),
                        preferred_element_type=jnp.float32) * HEAD_DIM ** (-0.5)
    probs = jnp.exp(scores - jnp.max(scores, axis=2, keepdims=True))
    total = jnp.sum(probs, axis=2)
    summed = jnp.einsum("qhk,khd->qhd", probs.astype(jnp.bfloat16), split(all_v),
                        preferred_element_type=jnp.float32)
    result = (summed / total[:, :, None]).reshape(heads_q.shape).astype(jnp.bfloat16)
    return lax.all_to_all(result, "uly", split_axis=0, concat_axis=1, tiled=True)


def solution(mesh):
    spec = P(("blk", "uly"), None)
    small = mesh.shape["blk"] == 2 * GROUPS and mesh.shape["uly"] == 4
    return jax.shard_map(
        attend if small else attend_any,
        mesh=mesh,
        in_specs=(spec, spec, spec),
        out_specs=spec,
        check_vma=False,
    )
```

```python
import functools

import jax
import jax.numpy as jnp
from jax import lax
from jax.experimental import pallas as pl
from jax.experimental.pallas import tpu as pltpu
from jax.sharding import PartitionSpec as P

HEAD_DIM = 128
GROUPS = 4
MESH = pl.DeviceIdType.MESH
LOG2E = 1.4426950408889634


def attend_kernel(q_in, k_in, v_in, out, q_buf, kv, o_buf, own_sem, keep_sem, z_send, z_recv, q_recv,
                  p_send, p_recv, f_send, f_recv, o_send, o_recv):
    rows, features = q_in.shape
    cols = features // GROUPS
    heads = cols // HEAD_DIM
    part = GROUPS * rows
    batches = head_batches(heads)
    b, u = lax.axis_index("blk"), lax.axis_index("uly")
    z, y = b // 2, b % 2
    x, c = u // 2, u % 2

    def plane(j):
        return lax.rem(z + j + GROUPS, GROUPS)

    def lanes(span):
        return pl.ds(span[0] * HEAD_DIM, (span[1] - span[0]) * HEAD_DIM)

    def column(index, span):
        start = pl.multiple_of(index * cols + span[0] * HEAD_DIM, HEAD_DIM)
        return pl.ds(start, (span[1] - span[0]) * HEAD_DIM)

    def piece(j):
        return pl.ds(j * rows, rows)

    others = pl.ds(rows, part - rows)
    x_peer = (b, 2 * (1 - x) + c)
    y_peer = (2 * z + 1 - y, u)
    sibling = (b, 2 * x + 1 - c)

    def z_peer(j):
        return (2 * plane(j) + y, u)

    sends = []

    def send(src, dst, send_sem, recv_sem, peer):
        copy = pltpu.make_async_remote_copy(
            src_ref=src, dst_ref=dst, send_sem=send_sem, recv_sem=recv_sem,
            device_id=peer, device_id_type=MESH)
        copy.start()
        sends.append(copy)

    def landed(ref, sem):
        pltpu.make_async_copy(ref, ref, sem).wait()

    every = (0, heads)
    own = [
        pltpu.make_async_copy(k_in.at[:, column(z, every)], kv.at[0, 0, piece(0)], own_sem.at[0]),
        pltpu.make_async_copy(v_in.at[:, column(z, every)], kv.at[1, 0, piece(0)], own_sem.at[1]),
        pltpu.make_async_copy(q_in.at[:, column(z, every)], q_buf.at[piece(0)], own_sem.at[2]),
    ]
    for copy in own:
        copy.start()

    barrier = pltpu.get_barrier_semaphore()
    peers = [z_peer(1), z_peer(2), z_peer(3), x_peer, y_peer, sibling]
    for peer in peers:
        pl.semaphore_signal(barrier, inc=1, device_id=peer, device_id_type=MESH)
    pl.semaphore_wait(barrier, len(peers))

    def send_keys(h):
        span = (h, h + 1)
        for j in range(1, GROUPS):
            away, base = column(plane(j), span), 9 * h + 3 * (j - 1)
            send(k_in.at[:, away], kv.at[0, 0, piece(j), lanes(span)], z_send.at[base], z_recv.at[h], z_peer(j))
            send(v_in.at[:, away], kv.at[1, 0, piece(j), lanes(span)], z_send.at[base + 1], z_recv.at[h], z_peer(j))

    def send_queries(h):
        span = (h, h + 1)
        for j in range(1, GROUPS):
            away, base = column(plane(j), span), 9 * h + 3 * (j - 1)
            send(q_in.at[:, away], q_buf.at[piece(j), lanes(span)], z_send.at[base + 2], q_recv.at[h], z_peer(j))

    def where(t):
        return (piece(0), lanes(every)) if t == 0 else (others, lanes(batches[t - 1]))

    def spread(t):
        at = where(t)
        if t == 0:
            own[0].wait()
            own[1].wait()
        else:
            landed(kv.at[:, 0, *at], z_recv.at[t - 1])
        for i, peer in ((0, x_peer), (1, y_peer)):
            send(kv.at[:, 0, *at], kv.at[:, i + 1, *at], p_send.at[4 * t + i], p_recv.at[4 * t + i], peer)
        send(kv.at[:, 0, *at], kv.at[:, 4, *at], f_send.at[4 * t], f_recv.at[t], sibling)

    def forward(t):
        at = where(t)
        for i, peer in ((0, y_peer), (1, x_peer)):
            landed(kv.at[:, i + 1, *at], p_recv.at[4 * t + i])
            send(kv.at[i, i + 1, *at], kv.at[i, 3, *at], p_send.at[4 * t + 2 + i], p_recv.at[4 * t + 2 + i], peer)
            send(kv.at[:, i + 1, *at], kv.at[:, i + 5, *at], f_send.at[4 * t + i + 1], f_recv.at[t], sibling)

    def finish(t):
        at = where(t)
        for i in range(2):
            landed(kv.at[i, 3, *at], p_recv.at[4 * t + 2 + i])
        send(kv.at[:, 3, *at], kv.at[:, 7, *at], f_send.at[4 * t + 3], f_recv.at[t], sibling)

    def gathered(t):
        landed(kv.at[:, pl.ds(4, 4), *where(t)], f_recv.at[t])

    keeps = []

    def fold(t):
        span = batches[t]
        if t == 0:
            own[2].wait()
            gathered(0)
        landed(q_buf.at[others, lanes(span)], q_recv.at[t])
        gathered(t + 1)
        for h in range(*span):
            one = lanes((h, h + 1))
            scores = lax.dot_general(
                q_buf[:, one], kv[0, :, :, one].reshape(8 * part, HEAD_DIM), (((1,), (1,)), ((), ())),
                preferred_element_type=jnp.float32)
            peak = jnp.max(scores, axis=1, keepdims=True)
            probs = jnp.exp2((scores - peak) * (LOG2E * HEAD_DIM ** -0.5))
            total = jnp.sum(probs, axis=1, keepdims=True)
            summed = jnp.dot(probs.astype(jnp.bfloat16), kv[1, :, :, one].reshape(8 * part, HEAD_DIM),
                             preferred_element_type=jnp.float32)
            o_buf[:, one] = (summed / total).astype(jnp.bfloat16)
        for j in range(1, GROUPS):
            send(o_buf.at[piece(j), lanes(span)], out.at[:, column(z, span)],
                 o_send.at[3 * t + j - 1], o_recv.at[j - 1], z_peer(-j))
        keep = pltpu.make_async_copy(o_buf.at[piece(0), lanes(span)], out.at[:, column(z, span)], keep_sem.at[t])
        keep.start()
        keeps.append(keep)

    last = heads
    steps = {"k": send_keys, "q": send_queries, "s": spread, "f": forward, "d": finish, "F": fold}
    for step in "k0 s0 k1 k2 k3 k4 q0 q1 q2 q3 q4 s1 s2 f0 s3 f1 s4 f2 d0 s5 f3 d1 f4 d2 F0 f5 d3 F1 d4 F2 d5 F3 F4".split():
        steps[step[0]](int(step[1:]))

    for keep in keeps:
        keep.wait()
    for j in range(1, GROUPS):
        landed(out.at[:, column(plane(j), every)], o_recv.at[j - 1])
    for copy in sends:
        copy.wait_send()


def head_batches(heads):
    return [(h, h + 1) for h in range(heads)]


def attend(queries, keys, values):
    rows, features = queries.shape
    cols = features // GROUPS
    heads = cols // HEAD_DIM
    part = GROUPS * rows
    count = len(head_batches(heads))
    dma = pltpu.SemaphoreType.DMA
    flops = 4 * part * cols * 8 * part
    return pl.pallas_call(
        attend_kernel,
        out_shape=jax.ShapeDtypeStruct((rows, features), jnp.bfloat16),
        in_specs=[pl.BlockSpec(memory_space=pl.ANY)] * 3,
        out_specs=pl.BlockSpec(memory_space=pl.ANY),
        scratch_shapes=[
            pltpu.VMEM((part, cols), jnp.bfloat16),
            pltpu.VMEM((2, 8, part, cols), jnp.bfloat16),
            pltpu.VMEM((part, cols), jnp.bfloat16),
            dma((3,)), dma((count,)), dma((9 * count,)), dma((count,)), dma((count,)),
            dma((4 * count + 4,)), dma((4 * count + 4,)), dma((4 * count + 4,)), dma((count + 1,)),
            dma((3 * count,)), dma((3,)),
        ],
        compiler_params=pltpu.CompilerParams(
            collective_id=0, has_side_effects=True, vmem_limit_bytes=60 * 2**20),
        cost_estimate=pl.CostEstimate(flops=flops, bytes_accessed=8 * rows * features, transcendentals=0),
    )(queries, keys, values)


def attend_any(queries, keys, values):
    def to_heads(array):
        return lax.all_to_all(array, "uly", split_axis=1, concat_axis=0, tiled=True)

    heads_q, heads_k, heads_v = to_heads(queries), to_heads(keys), to_heads(values)
    all_k = lax.all_gather(heads_k, "blk", axis=0, tiled=True)
    all_v = lax.all_gather(heads_v, "blk", axis=0, tiled=True)

    def split(array):
        return array.reshape(array.shape[0], -1, HEAD_DIM)

    scores = jnp.einsum("qhd,khd->qhk", split(heads_q), split(all_k),
                        preferred_element_type=jnp.float32) * HEAD_DIM ** (-0.5)
    probs = jnp.exp(scores - jnp.max(scores, axis=2, keepdims=True))
    total = jnp.sum(probs, axis=2)
    summed = jnp.einsum("qhk,khd->qhd", probs.astype(jnp.bfloat16), split(all_v),
                        preferred_element_type=jnp.float32)
    result = (summed / total[:, :, None]).reshape(heads_q.shape).astype(jnp.bfloat16)
    return lax.all_to_all(result, "uly", split_axis=0, concat_axis=1, tiled=True)


def solution(mesh):
    spec = P(("blk", "uly"), None)
    small = mesh.shape["blk"] == 2 * GROUPS and mesh.shape["uly"] == 4
    return jax.shard_map(
        attend if small else attend_any,
        mesh=mesh,
        in_specs=(spec, spec, spec),
        out_specs=spec,
        check_vma=False,
    )
```

```python
import functools

import jax
import jax.numpy as jnp
from jax import lax
from jax.experimental import pallas as pl
from jax.experimental.pallas import tpu as pltpu
from jax.sharding import PartitionSpec as P

HEAD_DIM = 128
GROUPS = 4
MESH = pl.DeviceIdType.MESH
LOG2E = 1.4426950408889634


def attend_kernel(q_in, k_in, v_in, out, q_buf, kv, o_buf, own_sem, keep_sem, z_send, z_recv, q_recv,
                  p_send, p_recv, f_send, f_recv, o_send, o_recv):
    rows, features = q_in.shape
    cols = features // GROUPS
    heads = cols // HEAD_DIM
    part = GROUPS * rows
    batches = head_batches(heads)
    b, u = lax.axis_index("blk"), lax.axis_index("uly")
    z, y = b // 2, b % 2
    x, c = u // 2, u % 2

    def plane(j):
        return lax.rem(z + j + GROUPS, GROUPS)

    def lanes(span):
        return pl.ds(span[0] * HEAD_DIM, (span[1] - span[0]) * HEAD_DIM)

    def column(index, span):
        start = pl.multiple_of(index * cols + span[0] * HEAD_DIM, HEAD_DIM)
        return pl.ds(start, (span[1] - span[0]) * HEAD_DIM)

    def piece(j):
        return pl.ds(j * rows, rows)

    others = pl.ds(rows, part - rows)
    x_peer = (b, 2 * (1 - x) + c)
    y_peer = (2 * z + 1 - y, u)
    d_peer = (2 * z + 1 - y, 2 * (1 - x) + c)
    sibling = (b, 2 * x + 1 - c)

    def z_peer(j):
        return (2 * plane(j) + y, u)

    sends = []

    def send(src, dst, send_sem, recv_sem, peer):
        copy = pltpu.make_async_remote_copy(
            src_ref=src, dst_ref=dst, send_sem=send_sem, recv_sem=recv_sem,
            device_id=peer, device_id_type=MESH)
        copy.start()
        sends.append(copy)

    def landed(ref, sem):
        pltpu.make_async_copy(ref, ref, sem).wait()

    every = (0, heads)
    own = [
        pltpu.make_async_copy(k_in.at[:, column(z, every)], kv.at[0, 0, piece(0)], own_sem.at[0]),
        pltpu.make_async_copy(v_in.at[:, column(z, every)], kv.at[1, 0, piece(0)], own_sem.at[1]),
        pltpu.make_async_copy(q_in.at[:, column(z, every)], q_buf.at[piece(0)], own_sem.at[2]),
    ]
    for copy in own:
        copy.start()

    barrier = pltpu.get_barrier_semaphore()
    peers = [z_peer(1), z_peer(2), z_peer(3), x_peer, y_peer, d_peer, sibling]
    for peer in peers:
        pl.semaphore_signal(barrier, inc=1, device_id=peer, device_id_type=MESH)
    pl.semaphore_wait(barrier, len(peers))

    def send_keys(h):
        span = (h, h + 1)
        for j in range(1, GROUPS):
            away, base = column(plane(j), span), 9 * h + 3 * (j - 1)
            send(k_in.at[:, away], kv.at[0, 0, piece(j), lanes(span)], z_send.at[base], z_recv.at[h], z_peer(j))
            send(v_in.at[:, away], kv.at[1, 0, piece(j), lanes(span)], z_send.at[base + 1], z_recv.at[h], z_peer(j))

    def send_queries(h):
        span = (h, h + 1)
        for j in range(1, GROUPS):
            away, base = column(plane(j), span), 9 * h + 3 * (j - 1)
            send(q_in.at[:, away], q_buf.at[piece(j), lanes(span)], z_send.at[base + 2], q_recv.at[h], z_peer(j))

    def where(t):
        return (piece(0), lanes(every)) if t == 0 else (others, lanes(batches[t - 1]))

    def straight(t):
        return t == heads

    def spread(t):
        at = where(t)
        if t == 0:
            own[0].wait()
            own[1].wait()
        else:
            landed(kv.at[:, 0, *at], z_recv.at[t - 1])
        for i, peer in ((0, x_peer), (1, y_peer)):
            send(kv.at[:, 0, *at], kv.at[:, i + 1, *at], p_send.at[4 * t + i], p_recv.at[4 * t + i], peer)
        if straight(t):
            send(kv.at[:, 0, *at], kv.at[:, 3, *at], p_send.at[4 * t + 2], p_recv.at[4 * t + 2], d_peer)
        send(kv.at[:, 0, *at], kv.at[:, 4, *at], f_send.at[4 * t], f_recv.at[t], sibling)

    def forward(t):
        at = where(t)
        for i, peer in ((0, y_peer), (1, x_peer)):
            landed(kv.at[:, i + 1, *at], p_recv.at[4 * t + i])
            if not straight(t):
                send(kv.at[i, i + 1, *at], kv.at[i, 3, *at], p_send.at[4 * t + 2 + i], p_recv.at[4 * t + 2 + i], peer)
            send(kv.at[:, i + 1, *at], kv.at[:, i + 5, *at], f_send.at[4 * t + i + 1], f_recv.at[t], sibling)

    def finish(t):
        at = where(t)
        if straight(t):
            landed(kv.at[:, 3, *at], p_recv.at[4 * t + 2])
        for i in range(0 if straight(t) else 2):
            landed(kv.at[i, 3, *at], p_recv.at[4 * t + 2 + i])
        send(kv.at[:, 3, *at], kv.at[:, 7, *at], f_send.at[4 * t + 3], f_recv.at[t], sibling)

    def gathered(t):
        landed(kv.at[:, pl.ds(4, 4), *where(t)], f_recv.at[t])

    keeps = []

    def fold(t):
        span = batches[t]
        if t == 0:
            own[2].wait()
            gathered(0)
        landed(q_buf.at[others, lanes(span)], q_recv.at[t])
        gathered(t + 1)
        for h in range(*span):
            one = lanes((h, h + 1))
            scores = lax.dot_general(
                q_buf[:, one], kv[0, :, :, one].reshape(8 * part, HEAD_DIM), (((1,), (1,)), ((), ())),
                preferred_element_type=jnp.float32)
            peak = jnp.max(scores, axis=1, keepdims=True)
            probs = jnp.exp2((scores - peak) * (LOG2E * HEAD_DIM ** -0.5))
            total = jnp.sum(probs, axis=1, keepdims=True)
            summed = jnp.dot(probs.astype(jnp.bfloat16), kv[1, :, :, one].reshape(8 * part, HEAD_DIM),
                             preferred_element_type=jnp.float32)
            o_buf[:, one] = (summed / total).astype(jnp.bfloat16)
        for j in range(1, GROUPS):
            send(o_buf.at[piece(j), lanes(span)], out.at[:, column(z, span)],
                 o_send.at[3 * t + j - 1], o_recv.at[j - 1], z_peer(-j))
        keep = pltpu.make_async_copy(o_buf.at[piece(0), lanes(span)], out.at[:, column(z, span)], keep_sem.at[t])
        keep.start()
        keeps.append(keep)

    last = heads
    steps = {"k": send_keys, "q": send_queries, "s": spread, "f": forward, "d": finish, "F": fold}
    order = ("k0", "s0", "k1", "k2", "k3", "k4", "q0", "q1", "q2", "q3", "q4", "s1", "s2",
             "f0", "s3", "f1", "s4", "f2", "d0", "s5", "f3", "d1", "f4", "d2", "F0", "f5", "d3", "F1",
             "d4", "d5", "F2", "F3", "F4")
    for step in order:
        steps[step[0]](int(step[1:]))

    for keep in keeps:
        keep.wait()
    for j in range(1, GROUPS):
        landed(out.at[:, column(plane(j), every)], o_recv.at[j - 1])
    for copy in sends:
        copy.wait_send()


def head_batches(heads):
    return [(h, h + 1) for h in range(heads)]


def attend(queries, keys, values):
    rows, features = queries.shape
    cols = features // GROUPS
    heads = cols // HEAD_DIM
    part = GROUPS * rows
    count = len(head_batches(heads))
    dma = pltpu.SemaphoreType.DMA
    flops = 4 * part * cols * 8 * part
    return pl.pallas_call(
        attend_kernel,
        out_shape=jax.ShapeDtypeStruct((rows, features), jnp.bfloat16),
        in_specs=[pl.BlockSpec(memory_space=pl.ANY)] * 3,
        out_specs=pl.BlockSpec(memory_space=pl.ANY),
        scratch_shapes=[
            pltpu.VMEM((part, cols), jnp.bfloat16),
            pltpu.VMEM((2, 8, part, cols), jnp.bfloat16),
            pltpu.VMEM((part, cols), jnp.bfloat16),
            dma((3,)), dma((count,)), dma((9 * count,)), dma((count,)), dma((count,)),
            dma((4 * count + 4,)), dma((4 * count + 4,)), dma((4 * count + 4,)), dma((count + 1,)),
            dma((3 * count,)), dma((3,)),
        ],
        compiler_params=pltpu.CompilerParams(
            collective_id=0, has_side_effects=True, vmem_limit_bytes=60 * 2**20),
        cost_estimate=pl.CostEstimate(flops=flops, bytes_accessed=8 * rows * features, transcendentals=0),
    )(queries, keys, values)


def attend_any(queries, keys, values):
    def to_heads(array):
        return lax.all_to_all(array, "uly", split_axis=1, concat_axis=0, tiled=True)

    heads_q, heads_k, heads_v = to_heads(queries), to_heads(keys), to_heads(values)
    all_k = lax.all_gather(heads_k, "blk", axis=0, tiled=True)
    all_v = lax.all_gather(heads_v, "blk", axis=0, tiled=True)

    def split(array):
        return array.reshape(array.shape[0], -1, HEAD_DIM)

    scores = jnp.einsum("qhd,khd->qhk", split(heads_q), split(all_k),
                        preferred_element_type=jnp.float32) * HEAD_DIM ** (-0.5)
    probs = jnp.exp(scores - jnp.max(scores, axis=2, keepdims=True))
    total = jnp.sum(probs, axis=2)
    summed = jnp.einsum("qhk,khd->qhd", probs.astype(jnp.bfloat16), split(all_v),
                        preferred_element_type=jnp.float32)
    result = (summed / total[:, :, None]).reshape(heads_q.shape).astype(jnp.bfloat16)
    return lax.all_to_all(result, "uly", split_axis=0, concat_axis=1, tiled=True)


def solution(mesh):
    spec = P(("blk", "uly"), None)
    small = mesh.shape["blk"] == 2 * GROUPS and mesh.shape["uly"] == 4
    return jax.shard_map(
        attend if small else attend_any,
        mesh=mesh,
        in_specs=(spec, spec, spec),
        out_specs=spec,
        check_vma=False,
    )
```

```python
import functools

import jax
import jax.numpy as jnp
from jax import lax
from jax.experimental import pallas as pl
from jax.experimental.pallas import tpu as pltpu
from jax.sharding import PartitionSpec as P

HEAD_DIM = 128
GROUPS = 4
MESH = pl.DeviceIdType.MESH
LOG2E = 1.4426950408889634


def attend_kernel(q_in, k_in, v_in, out, q_buf, kv, o_buf, own_sem, keep_sem, z_send, z_recv, q_recv,
                  p_send, p_recv, f_send, f_recv, o_send, o_recv):
    rows, features = q_in.shape
    cols = features // GROUPS
    heads = cols // HEAD_DIM
    part = GROUPS * rows
    batches = head_batches(heads)
    b, u = lax.axis_index("blk"), lax.axis_index("uly")
    z, y = b // 2, b % 2
    x, c = u // 2, u % 2

    def plane(j):
        return lax.rem(z + j + GROUPS, GROUPS)

    def lanes(span):
        return pl.ds(span[0] * HEAD_DIM, (span[1] - span[0]) * HEAD_DIM)

    def column(index, span):
        start = pl.multiple_of(index * cols + span[0] * HEAD_DIM, HEAD_DIM)
        return pl.ds(start, (span[1] - span[0]) * HEAD_DIM)

    def piece(j):
        return pl.ds(j * rows, rows)

    others = pl.ds(rows, part - rows)
    x_peer = (b, 2 * (1 - x) + c)
    y_peer = (2 * z + 1 - y, u)
    d_peer = (2 * z + 1 - y, 2 * (1 - x) + c)
    sibling = (b, 2 * x + 1 - c)

    def z_peer(j):
        return (2 * plane(j) + y, u)

    sends = []

    def send(src, dst, send_sem, recv_sem, peer):
        copy = pltpu.make_async_remote_copy(
            src_ref=src, dst_ref=dst, send_sem=send_sem, recv_sem=recv_sem,
            device_id=peer, device_id_type=MESH)
        copy.start()
        sends.append(copy)

    def landed(ref, sem):
        pltpu.make_async_copy(ref, ref, sem).wait()

    every = (0, heads)
    own = [
        pltpu.make_async_copy(k_in.at[:, column(z, every)], kv.at[0, 0, piece(0)], own_sem.at[0]),
        pltpu.make_async_copy(v_in.at[:, column(z, every)], kv.at[1, 0, piece(0)], own_sem.at[1]),
        pltpu.make_async_copy(q_in.at[:, column(z, every)], q_buf.at[piece(0)], own_sem.at[2]),
    ]
    barrier = pltpu.get_barrier_semaphore()
    peers = [z_peer(1), z_peer(2), z_peer(3), x_peer, y_peer, d_peer, sibling]
    for peer in peers:
        pl.semaphore_signal(barrier, inc=1, device_id=peer, device_id_type=MESH)
    for copy in own:
        copy.start()
    pl.semaphore_wait(barrier, len(peers))

    def send_keys(h):
        span = (h, h + 1)
        for j in range(1, GROUPS):
            away, base = column(plane(j), span), 9 * h + 3 * (j - 1)
            send(k_in.at[:, away], kv.at[0, 0, piece(j), lanes(span)], z_send.at[base], z_recv.at[h], z_peer(j))
            send(v_in.at[:, away], kv.at[1, 0, piece(j), lanes(span)], z_send.at[base + 1], z_recv.at[h], z_peer(j))

    def send_queries(h):
        span = (h, h + 1)
        for j in range(1, GROUPS):
            away, base = column(plane(j), span), 9 * h + 3 * (j - 1)
            send(q_in.at[:, away], q_buf.at[piece(j), lanes(span)], z_send.at[base + 2], q_recv.at[h], z_peer(j))

    def where(t):
        return (piece(0), lanes(every)) if t == 0 else (others, lanes(batches[t - 1]))

    def straight(t):
        return t == heads

    def spread(t):
        at = where(t)
        if t == 0:
            own[0].wait()
            own[1].wait()
        else:
            landed(kv.at[:, 0, *at], z_recv.at[t - 1])
        for i, peer in ((0, x_peer), (1, y_peer)):
            send(kv.at[:, 0, *at], kv.at[:, i + 1, *at], p_send.at[4 * t + i], p_recv.at[4 * t + i], peer)
        if straight(t):
            send(kv.at[:, 0, *at], kv.at[:, 3, *at], p_send.at[4 * t + 2], p_recv.at[4 * t + 2], d_peer)
        send(kv.at[:, 0, *at], kv.at[:, 4, *at], f_send.at[4 * t], f_recv.at[t], sibling)

    def forward(t):
        at = where(t)
        for i, peer in ((0, y_peer), (1, x_peer)):
            landed(kv.at[:, i + 1, *at], p_recv.at[4 * t + i])
            if not straight(t):
                send(kv.at[i, i + 1, *at], kv.at[i, 3, *at], p_send.at[4 * t + 2 + i], p_recv.at[4 * t + 2 + i], peer)
            send(kv.at[:, i + 1, *at], kv.at[:, i + 5, *at], f_send.at[4 * t + i + 1], f_recv.at[t], sibling)

    def finish(t):
        at = where(t)
        if straight(t):
            landed(kv.at[:, 3, *at], p_recv.at[4 * t + 2])
        for i in range(0 if straight(t) else 2):
            landed(kv.at[i, 3, *at], p_recv.at[4 * t + 2 + i])
        send(kv.at[:, 3, *at], kv.at[:, 7, *at], f_send.at[4 * t + 3], f_recv.at[t], sibling)

    def gathered(t):
        landed(kv.at[:, pl.ds(4, 4), *where(t)], f_recv.at[t])

    keeps = []

    def fold(t):
        span = batches[t]
        if t == 0:
            own[2].wait()
            gathered(0)
        landed(q_buf.at[others, lanes(span)], q_recv.at[t])
        gathered(t + 1)
        for h in range(*span):
            one = lanes((h, h + 1))
            scores = lax.dot_general(
                q_buf[:, one], kv[0, :, :, one].reshape(8 * part, HEAD_DIM), (((1,), (1,)), ((), ())),
                preferred_element_type=jnp.float32)
            peak = jnp.max(scores, axis=1, keepdims=True)
            probs = jnp.exp2((scores - peak) * (LOG2E * HEAD_DIM ** -0.5))
            total = jnp.sum(probs, axis=1, keepdims=True)
            summed = jnp.dot(probs.astype(jnp.bfloat16), kv[1, :, :, one].reshape(8 * part, HEAD_DIM),
                             preferred_element_type=jnp.float32)
            o_buf[:, one] = (summed / total).astype(jnp.bfloat16)
        for j in range(1, GROUPS):
            send(o_buf.at[piece(j), lanes(span)], out.at[:, column(z, span)],
                 o_send.at[3 * t + j - 1], o_recv.at[j - 1], z_peer(-j))
        keep = pltpu.make_async_copy(o_buf.at[piece(0), lanes(span)], out.at[:, column(z, span)], keep_sem.at[t])
        keep.start()
        keeps.append(keep)

    last = heads
    steps = {"k": send_keys, "q": send_queries, "s": spread, "f": forward, "d": finish, "F": fold}
    order = ("k0", "s0", "k1", "k2", "k3", "k4", "q0", "q1", "q2", "q3", "q4", "s1", "s2",
             "f0", "s3", "f1", "s4", "f2", "d0", "s5", "f3", "d1", "f4", "d2", "F0", "f5", "d3", "F1",
             "d4", "d5", "F2", "F3", "F4")
    for step in order:
        steps[step[0]](int(step[1:]))

    for keep in keeps:
        keep.wait()
    for j in range(1, GROUPS):
        landed(out.at[:, column(plane(j), every)], o_recv.at[j - 1])
    for copy in sends:
        copy.wait_send()


def head_batches(heads):
    return [(h, h + 1) for h in range(heads)]


def attend(queries, keys, values):
    rows, features = queries.shape
    cols = features // GROUPS
    heads = cols // HEAD_DIM
    part = GROUPS * rows
    count = len(head_batches(heads))
    dma = pltpu.SemaphoreType.DMA
    flops = 4 * part * cols * 8 * part
    return pl.pallas_call(
        attend_kernel,
        out_shape=jax.ShapeDtypeStruct((rows, features), jnp.bfloat16),
        in_specs=[pl.BlockSpec(memory_space=pl.ANY)] * 3,
        out_specs=pl.BlockSpec(memory_space=pl.ANY),
        scratch_shapes=[
            pltpu.VMEM((part, cols), jnp.bfloat16),
            pltpu.VMEM((2, 8, part, cols), jnp.bfloat16),
            pltpu.VMEM((part, cols), jnp.bfloat16),
            dma((3,)), dma((count,)), dma((9 * count,)), dma((count,)), dma((count,)),
            dma((4 * count + 4,)), dma((4 * count + 4,)), dma((4 * count + 4,)), dma((count + 1,)),
            dma((3 * count,)), dma((3,)),
        ],
        compiler_params=pltpu.CompilerParams(
            collective_id=0, has_side_effects=True, vmem_limit_bytes=60 * 2**20),
        cost_estimate=pl.CostEstimate(flops=flops, bytes_accessed=8 * rows * features, transcendentals=0),
    )(queries, keys, values)


def attend_any(queries, keys, values):
    def to_heads(array):
        return lax.all_to_all(array, "uly", split_axis=1, concat_axis=0, tiled=True)

    heads_q, heads_k, heads_v = to_heads(queries), to_heads(keys), to_heads(values)
    all_k = lax.all_gather(heads_k, "blk", axis=0, tiled=True)
    all_v = lax.all_gather(heads_v, "blk", axis=0, tiled=True)

    def split(array):
        return array.reshape(array.shape[0], -1, HEAD_DIM)

    scores = jnp.einsum("qhd,khd->qhk", split(heads_q), split(all_k),
                        preferred_element_type=jnp.float32) * HEAD_DIM ** (-0.5)
    probs = jnp.exp(scores - jnp.max(scores, axis=2, keepdims=True))
    total = jnp.sum(probs, axis=2)
    summed = jnp.einsum("qhk,khd->qhd", probs.astype(jnp.bfloat16), split(all_v),
                        preferred_element_type=jnp.float32)
    result = (summed / total[:, :, None]).reshape(heads_q.shape).astype(jnp.bfloat16)
    return lax.all_to_all(result, "uly", split_axis=0, concat_axis=1, tiled=True)


def solution(mesh):
    spec = P(("blk", "uly"), None)
    small = mesh.shape["blk"] == 2 * GROUPS and mesh.shape["uly"] == 4
    return jax.shard_map(
        attend if small else attend_any,
        mesh=mesh,
        in_specs=(spec, spec, spec),
        out_specs=spec,
        check_vma=False,
    )
```
